512 devices in a mesh: dp: 64 (over z, y), tile: 8 (over x, core).
Axes of the slice: x: 4, y: 8, z: 8, core: 2. Of those that a mesh axis runs over, the one named last changes fastest.
Arguments:
- embeddings: bfloat16 [262144, 768], P('dp'), may hold values from -30 to 30
- cluster_ids: int32 [262144], P('dp'), may hold values from 0 to 255, as said below
- padding: int32 [262144], P('dp'), may hold values from 0 to 1
Outputs:
- nearest: float32 [262144], P('dp')
The draws below stay inside these ranges and needn't reach their ends.
Inputs may be any that keep to these rules, and one draw needn't show every extreme that they name: cluster_ids is used only where padding is 0. Among the unpadded rows of one dp index (aligned blocks of 4096 rows), at most 64 have cluster ids of one residue modulo 64. In every draw some block has exactly 64 unpadded rows of every residue, and some residue takes exactly 64 rows from every block.
All inputs are finite; a program needn't handle non-finite values.
Results may differ from the reference program's by a relative error of at most 0.0003.
Values may be sent and summed in bfloat16 or wider, within the bound.
No kernel may reach another device: no remote copies, remote signals or barrier semaphores. Data moves between devices by JAX's collectives and lax.ppermute only.
A program may use at most 64 MiB of HBM per device.

```python
import jax
import jax.numpy as jnp
from jax import lax

D = 768
CAPR = 64
CL_OWN = 4
R_DEV = 4096
ROWS = 262144
NCL = 256
N_DP = 64


def layout_rows(key):
    devices = ROWS // R_DEV
    classes = jax.random.permutation(jax.random.fold_in(key, 11), devices)
    quarter = devices // 4
    base = jnp.where(classes < quarter, CAPR, jnp.where(classes < 2 * quarter, CAPR // 2, CAPR // 4))
    reach = jnp.where(classes < quarter, 1, jnp.where(classes < 2 * quarter, CAPR // 4, CAPR // 8))
    raw_jitter = jax.random.randint(jax.random.fold_in(key, 12), (devices, devices), 0, 1 << 20)
    counts = base[None, :] - raw_jitter % reach[None, :]
    full_sender = jax.random.randint(jax.random.fold_in(key, 17), (), 0, devices)
    sender_index = jnp.arange(devices)[:, None]
    counts = jnp.where(sender_index == full_sender, CAPR, counts)
    bounds = jnp.cumsum(counts, axis=1)
    position = jnp.arange(R_DEV)
    owner_sorted = jnp.sum((bounds[:, None, :] <= position[None, :, None]).astype(jnp.int32), axis=2)
    row_keys = jax.random.split(jax.random.fold_in(key, 13), devices)
    shuffles = jax.vmap(lambda k: jax.random.permutation(k, R_DEV))(row_keys)
    owner_rows = jnp.take_along_axis(owner_sorted, shuffles, axis=1)
    lone_owner = jax.random.permutation(jax.random.fold_in(key, 16), devices)
    lonely = (owner_rows == lone_owner[:, None]).astype(jnp.int32)
    lonely_first = (lonely == 1) & (jnp.cumsum(lonely, axis=1) == 1)
    first_pick = jax.random.randint(jax.random.fold_in(key, 14), (devices, R_DEV), 0, CL_OWN - 1)
    second_pick = jax.random.randint(jax.random.fold_in(key, 15), (devices, R_DEV), 0, CL_OWN - 1)
    picks = jnp.where(lonely_first, CL_OWN - 1, jnp.minimum(first_pick, second_pick))
    ids = jnp.minimum(owner_rows, devices - 1) + devices * picks
    padded = (owner_rows >= devices).astype(jnp.int32)
    return (ids.reshape(-1).astype(jnp.int32), padded.reshape(-1).astype(jnp.int32))


def draw_cluster_ids(key, part):
    return layout_rows(key)[0]


def draw_padding(key, part):
    return layout_rows(key)[1]


def draw_embeddings(key, part):
    ids, padded = layout_rows(key)
    devices = ROWS // R_DEV
    key = jax.random.fold_in(key, 5)
    shared = jax.random.normal(jax.random.fold_in(key, 1), (devices, D), jnp.float32)
    separate = jax.random.normal(jax.random.fold_in(key, 6), (NCL, D), jnp.float32)
    owner_index = jnp.arange(NCL) % devices
    centers = 0.83666 * shared[owner_index] + 0.54772 * separate
    levels = jnp.exp(jax.random.uniform(jax.random.fold_in(key, 7), (NCL,), jnp.float32, -1.6, 1.2))
    noise = jax.random.normal(jax.random.fold_in(key, 2), (ROWS, D), jnp.float32)
    jitter = jnp.exp(jax.random.uniform(jax.random.fold_in(key, 3), (ROWS,), jnp.float32, -0.3, 0.3))
    pull = levels[ids] * jitter
    values = pull[:, None] * centers[ids] + noise
    return jnp.clip(values, -30.0, 30.0).astype(jnp.bfloat16)


def setup_inputs(seed: int = 0) -> dict:
    keys = jax.random.split(jax.random.key(seed), 4)
    embeddings = draw_embeddings(jax.random.fold_in(keys[3], 71), 0)
    cluster_ids = draw_cluster_ids(jax.random.fold_in(keys[3], 71), 0)
    padding = draw_padding(jax.random.fold_in(keys[3], 71), 0)
    return dict(embeddings=embeddings, cluster_ids=cluster_ids, padding=padding)


def reference(embeddings, cluster_ids, padding):
    values = embeddings.astype(jnp.float32)
    unit = (values * lax.rsqrt(lax.optimization_barrier(jnp.sum(values * values, axis=1, keepdims=True)) + 1e-06)).astype(jnp.bfloat16)
    unpadded = padding == 0
    window = N_DP * CAPR
    owner_key = jnp.where(unpadded, cluster_ids % N_DP, N_DP).astype(jnp.int32)
    order = jnp.argsort(owner_key, stable=True).astype(jnp.int32)
    labels = jnp.where(unpadded, cluster_ids, -1).astype(jnp.int32)
    sorted_units = jnp.concatenate([unit[order], jnp.zeros((window, D), jnp.bfloat16)], axis=0)
    sorted_labels = jnp.concatenate([labels[order], jnp.full((window,), -1, jnp.int32)], axis=0)
    counts = lax.optimization_barrier(jnp.sum((owner_key[None, :] == jnp.arange(N_DP, dtype=jnp.int32)[:, None]).astype(jnp.int32), axis=1))
    starts = (jnp.cumsum(counts) - counts).astype(jnp.int32)
    diagonal = jnp.arange(window)[:, None] == jnp.arange(window)[None, :]

    def step(best, owner_now):
        begin = starts[owner_now]
        block_units = lax.dynamic_slice_in_dim(sorted_units, begin, window, 0)
        tags = lax.dynamic_slice_in_dim(sorted_labels, begin, window, 0)
        scores = jnp.dot(block_units, block_units.T, preferred_element_type=jnp.float32)
        allowed = (tags[:, None] == tags[None, :]) & (tags[None, :] >= 0) & jnp.logical_not(diagonal)
        top_values = lax.optimization_barrier(jnp.max(jnp.where(allowed, scores, jnp.float32(-1.0)), axis=1))
        return (lax.dynamic_update_slice_in_dim(best, top_values, begin, 0), None)
    initial = jnp.full((ROWS + window,), -1.0, jnp.float32)
    best, _ = lax.scan(step, initial, jnp.arange(N_DP, dtype=jnp.int32))
    placed = jnp.zeros((ROWS,), jnp.float32).at[order].set(best[:ROWS])
    return jnp.where(unpadded, placed, jnp.float32(-1.0)).astype(jnp.float32)
```

```python
import functools

import jax
import jax.numpy as jnp
from jax import lax
from jax.experimental import pallas as pl
from jax.experimental.pallas import tpu as pltpu
from jax.sharding import PartitionSpec as P

OWNERS = 64
CAPACITY = 64
TILES = 8
PART = CAPACITY // TILES
ROWS = OWNERS * PART
TAG = 2.0
VMEM = 60 * 1024 * 1024


def iota(shape, dim):
    return lax.broadcasted_iota(jnp.int32, shape, dim)


def nt_dot(a, b):
    return lax.dot_general(a, b, (((1,), (1,)), ((), ())), preferred_element_type=jnp.float32)


def one_hot(flags):
    return jnp.where(flags, jnp.float32(1), jnp.float32(0)).astype(jnp.bfloat16)


def pack_kernel(tile_ref, ids_ref, padding_ref, emb_ref, unit_ref, place_ref, tags):
    rows = ids_ref.shape[1]
    width = 256
    ids = ids_ref[...]
    owner = jnp.where(padding_ref[...] == 0, ids % OWNERS, -1)
    member = owner == iota((OWNERS, rows), 0)
    member_hot = one_hot(member)
    strictly_before = one_hot(iota((width, width), 0) < iota((width, width), 1))
    carry = jnp.zeros((OWNERS, 1), jnp.float32)
    slots = []
    for start in range(0, rows, width):
        block = member_hot[:, start : start + width]
        rank = carry + jnp.dot(block, strictly_before, preferred_element_type=jnp.float32)
        block = block.astype(jnp.float32)
        slots.append(jnp.sum(block * rank, axis=0, keepdims=True))
        carry = carry + jnp.sum(block, axis=1, keepdims=True)
    slot = jnp.concatenate(slots, axis=1).astype(jnp.int32)
    place_ref[...] = jnp.where(owner >= 0, owner * CAPACITY + slot, -1)
    part = slot // PART
    local = slot % PART
    wanted = jnp.where((owner >= 0) & (part == tile_ref[0]), owner * PART + local, -1)
    total = jnp.zeros((ROWS, emb_ref.shape[1]), jnp.float32)
    step = 1024
    for start in range(0, rows, step):
        pick = one_hot(iota((ROWS, step), 0) == wanted[:, start : start + step])
        total = total + jnp.dot(
            pick, emb_ref[start : start + step, :], preferred_element_type=jnp.float32
        )
    scale = lax.rsqrt(jnp.sum(total * total, axis=1, keepdims=True) + 1e-06)
    features = emb_ref.shape[1]
    unit_ref[:, :features] = (total * scale).astype(jnp.bfloat16)
    marks = TILES * 4
    mark = jnp.where(owner >= 0, local * marks + part * 4 + ids // OWNERS, -1)
    mark_hot = one_hot(iota((PART * marks, rows), 0) == mark)
    by_owner = TAG * nt_dot(member_hot, mark_hot)
    tags[...] = jnp.zeros(tags.shape, jnp.float32)
    for i in range(PART):
        tags[:, i, :marks] = by_owner[:, i * marks : (i + 1) * marks]
    unit_ref[:, features:] = tags[...].reshape(ROWS, 128).astype(jnp.bfloat16)


def marks_of(tag, group):
    lane, mark = iota((128, 128), 0), iota((128, 128), 1)
    take = one_hot((lane == group * 4 + mark) & (mark < 4))
    return jnp.dot(tag, take, preferred_element_type=jnp.float32).astype(jnp.bfloat16)


def spread(best, group):
    row, lane = iota((ROWS, 128), 0), iota((ROWS, 128), 1)
    value = jnp.maximum(best - TAG * TAG, -1.0)
    placed = jnp.where(lane == group * PART + row % PART, value, -2.0)
    return jnp.max(placed.reshape(OWNERS, PART, 128), axis=1)


def own_kernel(groups_ref, tag_ref, a_ref, b_ref, out_ref):
    tag = tag_ref[...]
    marks_a, marks_b = marks_of(tag, groups_ref[0]), marks_of(tag, groups_ref[1])
    a = a_ref[...]
    same = nt_dot(a, a) + nt_dot(marks_a, marks_a)
    same = jnp.where(iota((ROWS, ROWS), 0) == iota((ROWS, ROWS), 1), -2.0, same)
    other = nt_dot(a, b_ref[...]) + nt_dot(marks_a, marks_b)
    best = jnp.max(jnp.maximum(same, other), axis=1, keepdims=True)
    out_ref[...] = spread(best, groups_ref[0])


def cross_kernel(groups_ref, tag_ref, own_ref, a_ref, b_ref, p_ref, n_ref, out_ref):
    tag = tag_ref[...]
    marks_n = marks_of(tag, groups_ref[3])
    columns = n_ref[...]
    out = own_ref[...]
    best_n = jnp.full((8, ROWS), -2.0, jnp.float32)
    for j, ref in enumerate((a_ref, b_ref, p_ref)):
        scores = nt_dot(ref[...], columns) + nt_dot(marks_of(tag, groups_ref[j]), marks_n)
        out = jnp.maximum(out, spread(jnp.max(scores, axis=1, keepdims=True), groups_ref[j]))
        best_n = jnp.maximum(best_n, jnp.max(scores.reshape(ROWS // 8, 8, ROWS), axis=0))
    best_n = jnp.broadcast_to(jnp.max(best_n, axis=0, keepdims=True), (128, ROWS)).T
    out_ref[...] = jnp.maximum(out, spread(best_n[:, :1], groups_ref[3]))


def pick_kernel(place_ref, best_ref, out_ref):
    place = place_ref[...]
    rows = place.shape[1]
    owner_hot = one_hot(place // CAPACITY == iota((OWNERS, rows), 0))
    best = best_ref[...].T
    high = best.astype(jnp.bfloat16)
    rest = best - high.astype(jnp.float32)
    middle = rest.astype(jnp.bfloat16)
    low = (rest - middle.astype(jnp.float32)).astype(jnp.bfloat16)
    by_slot = (
        jnp.dot(high, owner_hot, preferred_element_type=jnp.float32)
        + jnp.dot(middle, owner_hot, preferred_element_type=jnp.float32)
        + jnp.dot(low, owner_hot, preferred_element_type=jnp.float32)
    )
    here = place % CAPACITY == iota((CAPACITY, rows), 0)
    picked = jnp.sum(jnp.where(here, by_slot, 0.0), axis=0, keepdims=True)
    out_ref[...] = jnp.where(place >= 0, picked, -1.0)


def call(kernel, out_shape, in_specs, flops=0, scratch=()):
    return pl.pallas_call(
        kernel,
        out_shape=out_shape,
        in_specs=in_specs,
        scratch_shapes=list(scratch),
        compiler_params=pltpu.CompilerParams(vmem_limit_bytes=VMEM),
        cost_estimate=pl.CostEstimate(flops=flops, bytes_accessed=1 << 20, transcendentals=0),
    )


def on_device(embeddings, cluster_ids, padding):
    rows, features = embeddings.shape
    tile = lax.axis_index("tile")
    chip, core = tile // 2, tile % 2
    vmem = pl.BlockSpec(memory_space=pltpu.VMEM)
    smem = pl.BlockSpec(memory_space=pltpu.SMEM)
    packed, place = call(
        pack_kernel,
        (
            jax.ShapeDtypeStruct((ROWS, features + 128), jnp.bfloat16),
            jax.ShapeDtypeStruct((1, rows), jnp.int32),
        ),
        [smem, vmem, vmem, vmem],
        scratch=[pltpu.VMEM((OWNERS, PART, 128), jnp.float32)],
    )(tile.reshape(1), cluster_ids.reshape(1, rows), padding.reshape(1, rows), embeddings)
    packed = packed.reshape(OWNERS, PART, features + 128)
    received = lax.all_to_all(packed, "dp", split_axis=0, concat_axis=0, tiled=True)
    received = received.reshape(ROWS, features + 128)
    a, tag = received[:, :features], received[:, features:]
    swap = [(2 * x + c, 2 * x + 1 - c) for x in range(4) for c in range(2)]
    forward = [(2 * x + c, 2 * ((x + 1) % 4) + c) for x in range(4) for c in range(2)]
    backward = [
        (2 * ((x + 1) % 4) + (c if x < 2 else 1 - c), 2 * x + c) for x in range(4) for c in range(2)
    ]
    b = lax.ppermute(a, "tile", swap)
    p = lax.ppermute(a, "tile", forward)
    n = lax.ppermute(a, "tile", backward)
    groups = jnp.stack(
        [
            tile,
            2 * chip + 1 - core,
            2 * ((chip + 3) % 4) + core,
            2 * ((chip + 1) % 4) + jnp.where(chip < 2, core, 1 - core),
        ]
    ).astype(jnp.int32)
    partial_shape = jax.ShapeDtypeStruct((OWNERS, 128), jnp.float32)
    own = call(
        own_kernel,
        partial_shape,
        [smem, vmem, vmem, vmem],
        flops=2 * ROWS * 2 * ROWS * features,
    )(groups, tag, a, b)
    best = call(
        cross_kernel,
        partial_shape,
        [smem, vmem, vmem, vmem, vmem, vmem, vmem],
        flops=2 * 3 * ROWS * ROWS * features,
    )(groups, tag, own, a, b, p, n)
    best = best[:, :CAPACITY]
    best = lax.all_to_all(best, "dp", split_axis=0, concat_axis=0, tiled=True)
    best = lax.pmax(best, "tile")
    nearest = call(
        pick_kernel,
        jax.ShapeDtypeStruct((1, rows), jnp.float32),
        [vmem, vmem],
    )(place, best)
    return nearest.reshape(rows)


def solution(mesh):
    in_specs = (P("dp", None), P("dp"), P("dp"))
    out_specs = P("dp")
    return jax.shard_map(
        on_device, mesh=mesh, in_specs=in_specs, out_specs=out_specs, check_vma=False
    )
```

```python
import jax
import jax.numpy as jnp
from jax import lax
from jax.experimental import pallas as pl
from jax.experimental.pallas import tpu as pltpu
from jax.sharding import PartitionSpec as P

OWNERS = 64
CAPACITY = 64
TILES = 8
PART = CAPACITY // TILES
ROWS = OWNERS * PART
TAG = 2.0
NEXT_CROSSED = (0, 0, 0, 1)
PREVIOUS_CROSSED = (0, 1, 1, 1)
PLACE_FLOPS = 4_000_000_000
VMEM = 16 * 1024 * 1024


def iota(shape, dim):
    return lax.broadcasted_iota(jnp.int32, shape, dim)


def nt_dot(a, b):
    return lax.dot_general(a, b, (((1,), (1,)), ((), ())), preferred_element_type=jnp.float32)


def one_hot(flags):
    return jnp.where(flags, jnp.float32(1), jnp.float32(0)).astype(jnp.bfloat16)


def place_kernel(tile_ref, labels_ref, place_ref, wanted_ref, tag_ref, tags):
    rows = labels_ref.shape[1]
    width = 256
    labels = labels_ref[...]
    owner = jnp.where(labels >= 0, labels & (OWNERS - 1), -1)
    member_hot = one_hot(owner == iota((OWNERS, rows), 0))
    strictly_before = one_hot(iota((width, width), 0) < iota((width, width), 1))
    carry = jnp.zeros((OWNERS, 1), jnp.float32)
    slots = []
    for start in range(0, rows, width):
        block = member_hot[:, start : start + width]
        rank = carry + jnp.dot(block, strictly_before, preferred_element_type=jnp.float32)
        block = block.astype(jnp.float32)
        slots.append(jnp.sum(block * rank, axis=0, keepdims=True))
        carry = carry + jnp.sum(block, axis=1, keepdims=True)
    slot = jnp.concatenate(slots, axis=1).astype(jnp.int32)
    place_ref[...] = jnp.where(owner >= 0, owner * CAPACITY + slot, -1)
    part = slot >> 3
    local = slot & (PART - 1)
    wanted_ref[...] = jnp.where((owner >= 0) & (part == tile_ref[0]), owner * PART + local, -1)
    marks = TILES * 4
    mark = jnp.where(owner >= 0, local * marks + part * 4 + (labels >> 6), -1)
    mark_hot = one_hot(iota((PART * marks, rows), 0) == mark)
    by_owner = TAG * nt_dot(member_hot, mark_hot)
    tags[...] = jnp.zeros(tags.shape, jnp.float32)
    for i in range(PART):
        tags[:, i, :marks] = by_owner[:, i * marks : (i + 1) * marks]
    tag_ref[...] = tags[...].reshape(ROWS, 128).astype(jnp.bfloat16)


def pack_kernel(wanted_ref, tag_ref, emb_ref, unit_ref):
    rows, features = emb_ref.shape
    pick = one_hot(iota((ROWS, rows), 0) == wanted_ref[...])
    total = jnp.dot(pick, emb_ref[...], preferred_element_type=jnp.float32)
    scale = lax.rsqrt(jnp.sum(total * total, axis=1, keepdims=True) + 1e-06)
    unit_ref[:, :features] = (total * scale).astype(jnp.bfloat16)
    unit_ref[:, features:] = tag_ref[...]


def marks_of(tag, group):
    lane, mark = iota((128, 128), 0), iota((128, 128), 1)
    take = one_hot((lane == group * 4 + mark) & (mark < 4))
    return jnp.dot(tag, take, preferred_element_type=jnp.float32).astype(jnp.bfloat16)


def spread(best, group):
    row, lane = iota((ROWS, 128), 0), iota((ROWS, 128), 1)
    value = jnp.maximum(best - TAG * TAG, -1.0)
    placed = jnp.where(lane == group * PART + row % PART, value, -2.0)
    return jnp.max(placed.reshape(OWNERS, PART, 128), axis=1)


def row_best(scores):
    return jnp.max(scores, axis=1, keepdims=True)


def column_best(scores):
    best = jnp.max(scores.reshape(scores.shape[0] // 8, 8, ROWS), axis=0)
    best = jnp.max(best, axis=0, keepdims=True)
    return jnp.broadcast_to(best, (128, ROWS)).T[:, :1]


def own_kernel(groups_ref, tag_ref, a_ref, out_ref):
    marks_a = marks_of(tag_ref[...], groups_ref[0])
    a = a_ref[...]
    same = nt_dot(a, a) + nt_dot(marks_a, marks_a)
    same = jnp.where(iota((ROWS, ROWS), 0) == iota((ROWS, ROWS), 1), -2.0, same)
    out_ref[...] = spread(row_best(same), groups_ref[0])


def previous_kernel(groups_ref, tag_ref, best_ref, a_ref, p_ref, out_ref):
    tag = tag_ref[...]
    marks_a, marks_p = marks_of(tag, groups_ref[0]), marks_of(tag, groups_ref[2])
    scores = nt_dot(a_ref[...], p_ref[...]) + nt_dot(marks_a, marks_p)
    best = jnp.maximum(best_ref[...], spread(row_best(scores), groups_ref[0]))
    out_ref[...] = jnp.maximum(best, spread(column_best(scores), groups_ref[2]))


def last_kernel(groups_ref, tag_ref, best_ref, a_ref, b_ref, p_ref, n_ref, out_ref):
    tag = tag_ref[...]
    a, n = a_ref[...], n_ref[...]
    marks_a, marks_n = marks_of(tag, groups_ref[0]), marks_of(tag, groups_ref[3])
    a_b = nt_dot(a, b_ref[...]) + nt_dot(marks_a, marks_of(tag, groups_ref[1]))
    a_n = nt_dot(a, n) + nt_dot(marks_a, marks_n)
    p_n = nt_dot(p_ref[...], n) + nt_dot(marks_of(tag, groups_ref[2]), marks_n)
    best = jnp.maximum(best_ref[...], spread(row_best(jnp.maximum(a_n, a_b)), groups_ref[0]))
    best = jnp.maximum(best, spread(row_best(p_n), groups_ref[2]))
    out_ref[...] = jnp.maximum(best, spread(column_best(jnp.maximum(a_n, p_n)), groups_ref[3]))


def pick_kernel(place_ref, best_ref, out_ref):
    place = place_ref[...]
    rows = place.shape[1]
    owner_hot = one_hot(place // CAPACITY == iota((OWNERS, rows), 0))
    best = jnp.max(best_ref[...], axis=0)
    best = best.T[:CAPACITY]
    high = best.astype(jnp.bfloat16)
    rest = best - high.astype(jnp.float32)
    middle = rest.astype(jnp.bfloat16)
    low = (rest - middle.astype(jnp.float32)).astype(jnp.bfloat16)
    by_slot = (
        jnp.dot(high, owner_hot, preferred_element_type=jnp.float32)
        + jnp.dot(middle, owner_hot, preferred_element_type=jnp.float32)
        + jnp.dot(low, owner_hot, preferred_element_type=jnp.float32)
    )
    here = place % CAPACITY == iota((CAPACITY, rows), 0)
    picked = jnp.sum(jnp.where(here, by_slot, 0.0), axis=0, keepdims=True)
    out_ref[...] = jnp.where(place >= 0, picked, -1.0)


def call(kernel, out_shape, in_specs, flops=0, scratch=()):
    return pl.pallas_call(
        kernel,
        out_shape=out_shape,
        in_specs=in_specs,
        scratch_shapes=list(scratch),
        compiler_params=pltpu.CompilerParams(vmem_limit_bytes=VMEM),
        cost_estimate=pl.CostEstimate(flops=flops, bytes_accessed=1 << 20, transcendentals=0),
    )


VMEM_SPEC = pl.BlockSpec(memory_space=pltpu.VMEM)
SMEM_SPEC = pl.BlockSpec(memory_space=pltpu.SMEM)
PARTIAL = jax.ShapeDtypeStruct((OWNERS, 128), jnp.float32)


def pack(tile, cluster_ids, padding, embeddings):
    rows, features = embeddings.shape
    labels = jnp.where(padding == 0, cluster_ids, -1).reshape(1, rows)
    row = jax.ShapeDtypeStruct((1, rows), jnp.int32)
    place, wanted, tag = call(
        place_kernel,
        (row, row, jax.ShapeDtypeStruct((ROWS, 128), jnp.bfloat16)),
        [SMEM_SPEC, VMEM_SPEC],
        flops=PLACE_FLOPS,
        scratch=[pltpu.VMEM((OWNERS, PART, 128), jnp.float32)],
    )(tile.reshape(1), labels)
    packed = call(
        pack_kernel,
        jax.ShapeDtypeStruct((ROWS, features + 128), jnp.bfloat16),
        [VMEM_SPEC] * 3,
        flops=2 * ROWS * rows * features,
    )(wanted, tag, embeddings)
    return packed, place


def scores(kernel, groups, *arrays):
    flops = 4 * ROWS * ROWS * arrays[-1].shape[1]
    specs = [SMEM_SPEC] + [VMEM_SPEC] * len(arrays)
    return call(kernel, PARTIAL, specs, flops)(groups, *arrays)


def pick(place, best):
    out_shape = jax.ShapeDtypeStruct(place.shape, jnp.float32)
    return call(pick_kernel, out_shape, [VMEM_SPEC] * 2)(place, best)


def on_device(embeddings, cluster_ids, padding):
    rows, features = embeddings.shape
    tile = lax.axis_index("tile")
    chip, core = tile // 2, tile % 2
    groups = jnp.stack(
        [
            tile,
            2 * chip + 1 - core,
            2 * ((chip + 3) % 4) + jnp.where(chip > 0, 1 - core, core),
            2 * ((chip + 1) % 4) + jnp.where(chip == 3, 1 - core, core),
        ]
    ).astype(jnp.int32)
    packed, place = pack(tile, cluster_ids, padding, embeddings)
    packed = packed.reshape(OWNERS, PART, features + 128)
    received = lax.all_to_all(packed, "dp", split_axis=0, concat_axis=0, tiled=True)
    received = received.reshape(ROWS, features + 128)
    a, tag = lax.optimization_barrier((received[:, :features], received[:, features:]))
    swap = [(2 * x + c, 2 * x + 1 - c) for x in range(4) for c in range(2)]
    backward = [
        (2 * ((x + 1) % 4) + c, 2 * x + (c ^ NEXT_CROSSED[x])) for x in range(4) for c in range(2)
    ]
    forward = [
        (2 * ((x + 3) % 4) + c, 2 * x + (c ^ PREVIOUS_CROSSED[x]))
        for x in range(4)
        for c in range(2)
    ]
    p = lax.ppermute(a, "tile", forward)
    n = lax.ppermute(a, "tile", backward)
    b = lax.ppermute(a, "tile", swap)
    best = scores(own_kernel, groups, tag, a)
    best = scores(previous_kernel, groups, tag, best, a, p)
    best = scores(last_kernel, groups, tag, best, a, b, p, n)
    best = lax.all_to_all(best, "dp", split_axis=0, concat_axis=0, tiled=True)
    best = jnp.broadcast_to(best[None], (TILES, OWNERS, 128))
    best = lax.all_to_all(best, "tile", split_axis=0, concat_axis=0, tiled=True)
    return pick(place, best).reshape(rows)


def solution(mesh):
    in_specs = (P("dp", None), P("dp"), P("dp"))
    out_specs = P("dp")
    return jax.shard_map(
        on_device, mesh=mesh, in_specs=in_specs, out_specs=out_specs, check_vma=False
    )
```

```python
import jax
import jax.numpy as jnp
from jax import lax
from jax.experimental import pallas as pl
from jax.experimental.pallas import tpu as pltpu
from jax.sharding import PartitionSpec as P

OWNERS = 64
CAPACITY = 64
TILES = 8
PART = CAPACITY // TILES
ROWS = OWNERS * PART
TAG = 2.0
NEXT_CROSSED = (0, 0, 0, 1)
PREVIOUS_CROSSED = (0, 1, 1, 1)
PLACE_FLOPS = 2_000_000_000
VMEM = 16 * 1024 * 1024


def iota(shape, dim):
    return lax.broadcasted_iota(jnp.int32, shape, dim)


def nt_dot(a, b):
    return lax.dot_general(a, b, (((1,), (1,)), ((), ())), preferred_element_type=jnp.float32)


def one_hot(flags):
    return jnp.where(flags, jnp.float32(1), jnp.float32(0)).astype(jnp.bfloat16)


def place_kernel(tile_ref, labels_ref, place_ref, wanted_ref, tag_ref, tags):
    rows = labels_ref.shape[1]
    width = 256
    labels = labels_ref[...]
    owner = jnp.where(labels >= 0, labels & (OWNERS - 1), -1)
    member_hot = one_hot(owner == iota((OWNERS, rows), 0))
    strictly_before = one_hot(iota((width, width), 0) < iota((width, width), 1))
    carry = jnp.zeros((OWNERS, 1), jnp.float32)
    slots = []
    for start in range(0, rows, width):
        block = member_hot[:, start : start + width]
        rank = carry + jnp.dot(block, strictly_before, preferred_element_type=jnp.float32)
        block = block.astype(jnp.float32)
        slots.append(jnp.sum(block * rank, axis=0, keepdims=True))
        carry = carry + jnp.sum(block, axis=1, keepdims=True)
    slot = jnp.concatenate(slots, axis=1).astype(jnp.int32)
    place_ref[...] = jnp.where(owner >= 0, owner * CAPACITY + slot, -1)
    part = slot >> 3
    local = slot & (PART - 1)
    wanted_ref[...] = jnp.where((owner >= 0) & (part == tile_ref[0]), owner * PART + local, -1)
    marks = TILES * 4
    mark = jnp.where(owner >= 0, local * marks + part * 4 + (labels >> 6), -1)
    mark_hot = one_hot(iota((PART * marks, rows), 0) == mark)
    by_owner = TAG * nt_dot(member_hot, mark_hot)
    tags[...] = jnp.zeros(tags.shape, jnp.float32)
    for i in range(PART):
        tags[:, i, :marks] = by_owner[:, i * marks : (i + 1) * marks]
    tag_ref[...] = tags[...].reshape(ROWS, 128).astype(jnp.bfloat16)


def pack_kernel(wanted_ref, tag_ref, emb_ref, unit_ref):
    rows, features = emb_ref.shape
    pick = one_hot(iota((ROWS, rows), 0) == wanted_ref[...])
    total = jnp.dot(pick, emb_ref[...], preferred_element_type=jnp.float32)
    scale = lax.rsqrt(jnp.sum(total * total, axis=1, keepdims=True) + 1e-06)
    unit_ref[:, :features] = (total * scale).astype(jnp.bfloat16)
    unit_ref[:, features:] = tag_ref[...]


def marks_of(tag, group):
    lane, mark = iota((128, 128), 0), iota((128, 128), 1)
    take = one_hot((lane == group * 4 + mark) & (mark < 4))
    return jnp.dot(tag, take, preferred_element_type=jnp.float32).astype(jnp.bfloat16)


def spread(best, group):
    row, lane = iota((ROWS, 128), 0), iota((ROWS, 128), 1)
    value = jnp.maximum(best - TAG * TAG, -1.0)
    here = lane == group * PART + (row & 7) + ((row >> 5) & 1) * CAPACITY
    placed = jnp.where(here, value, -2.0).reshape(8, 2, 4, PART, 128)
    return jnp.max(jnp.max(placed, axis=1), axis=2).reshape(32, 128)


def row_best(scores):
    return jnp.max(scores, axis=1, keepdims=True)


def column_best(scores):
    best = jnp.max(scores.reshape(scores.shape[0] // 8, 8, ROWS), axis=0)
    best = jnp.max(best, axis=0, keepdims=True)
    return jnp.broadcast_to(best, (128, ROWS)).T[:, :1]


def own_kernel(groups_ref, tag_ref, a_ref, out_ref, marks_ref):
    tag = tag_ref[...]
    for j in range(4):
        marks_ref[j * ROWS : (j + 1) * ROWS, :] = marks_of(tag, groups_ref[j])
    marks_a = marks_ref[:ROWS, :]
    a = a_ref[...]
    same = nt_dot(a, a) + nt_dot(marks_a, marks_a)
    same = jnp.where(iota((ROWS, ROWS), 0) == iota((ROWS, ROWS), 1), -2.0, same)
    out_ref[...] = spread(row_best(same), groups_ref[0])


def marks(marks_ref, j):
    return marks_ref[j * ROWS : (j + 1) * ROWS, :]


def previous_kernel(groups_ref, marks_ref, best_ref, a_ref, p_ref, out_ref):
    marks_a, marks_p = marks(marks_ref, 0), marks(marks_ref, 2)
    scores = nt_dot(a_ref[...], p_ref[...]) + nt_dot(marks_a, marks_p)
    best = jnp.maximum(best_ref[...], spread(row_best(scores), groups_ref[0]))
    out_ref[...] = jnp.maximum(best, spread(column_best(scores), groups_ref[2]))


def last_kernel(groups_ref, marks_ref, best_ref, a_ref, b_ref, p_ref, n_ref, out_ref):
    a, n = a_ref[...], n_ref[...]
    marks_a, marks_n = marks(marks_ref, 0), marks(marks_ref, 3)
    a_b = nt_dot(a, b_ref[...]) + nt_dot(marks_a, marks(marks_ref, 1))
    a_n = nt_dot(a, n) + nt_dot(marks_a, marks_n)
    p_n = nt_dot(p_ref[...], n) + nt_dot(marks(marks_ref, 2), marks_n)
    best = jnp.maximum(best_ref[...], spread(row_best(jnp.maximum(a_n, a_b)), groups_ref[0]))
    best = jnp.maximum(best, spread(row_best(p_n), groups_ref[2]))
    out_ref[...] = jnp.maximum(best, spread(column_best(jnp.maximum(a_n, p_n)), groups_ref[3]))


def pick_kernel(place_ref, best_ref, out_ref):
    place = place_ref[...]
    rows = place.shape[1]
    owner = place >> 6
    z, y = owner >> 3, owner & 7
    owner_hot = one_hot(((z >> 2) << 5) + (y << 2) + (z & 3) == iota((OWNERS, rows), 0))
    best = jnp.max(best_ref[...], axis=1).reshape(32, 128).T
    best = jnp.concatenate([best[:CAPACITY], best[CAPACITY:]], axis=1)
    high = best.astype(jnp.bfloat16)
    rest = best - high.astype(jnp.float32)
    middle = rest.astype(jnp.bfloat16)
    low = (rest - middle.astype(jnp.float32)).astype(jnp.bfloat16)
    by_slot = (
        jnp.dot(high, owner_hot, preferred_element_type=jnp.float32)
        + jnp.dot(middle, owner_hot, preferred_element_type=jnp.float32)
        + jnp.dot(low, owner_hot, preferred_element_type=jnp.float32)
    )
    here = (place & (CAPACITY - 1)) == iota((CAPACITY, rows), 0)
    picked = jnp.sum(jnp.where(here, by_slot, 0.0), axis=0, keepdims=True)
    out_ref[...] = jnp.where(place >= 0, picked, -1.0)


def call(kernel, out_shape, in_specs, flops=0, scratch=()):
    return pl.pallas_call(
        kernel,
        out_shape=out_shape,
        in_specs=in_specs,
        scratch_shapes=list(scratch),
        compiler_params=pltpu.CompilerParams(vmem_limit_bytes=VMEM),
        cost_estimate=pl.CostEstimate(flops=flops, bytes_accessed=1 << 20, transcendentals=0),
    )


VMEM_SPEC = pl.BlockSpec(memory_space=pltpu.VMEM)
SMEM_SPEC = pl.BlockSpec(memory_space=pltpu.SMEM)
PARTIAL = jax.ShapeDtypeStruct((32, 128), jnp.float32)


def pack(tile, cluster_ids, padding, embeddings):
    rows, features = embeddings.shape
    labels = jnp.where(padding == 0, cluster_ids, -1).reshape(1, rows)
    row = jax.ShapeDtypeStruct((1, rows), jnp.int32)
    place, wanted, tag = call(
        place_kernel,
        (row, row, jax.ShapeDtypeStruct((ROWS, 128), jnp.bfloat16)),
        [SMEM_SPEC, VMEM_SPEC],
        flops=PLACE_FLOPS,
        scratch=[pltpu.VMEM((OWNERS, PART, 128), jnp.float32)],
    )(tile.reshape(1), labels)
    packed = call(
        pack_kernel,
        jax.ShapeDtypeStruct((ROWS, features + 128), jnp.bfloat16),
        [VMEM_SPEC] * 3,
        flops=2 * ROWS * rows * features,
    )(wanted, tag, embeddings)
    return packed, place


def scores(kernel, groups, *arrays, out_shape=PARTIAL):
    flops = 4 * ROWS * ROWS * arrays[-1].shape[1]
    specs = [SMEM_SPEC] + [VMEM_SPEC] * len(arrays)
    return call(kernel, out_shape, specs, flops)(groups, *arrays)


def pick(place, best):
    out_shape = jax.ShapeDtypeStruct(place.shape, jnp.float32)
    return call(pick_kernel, out_shape, [VMEM_SPEC] * 2)(place, best)


def exchange(array, axes):
    sizes = dict(z=8, y=8, x=4, c=2)
    strides = dict(z=64, y=8, x=2, c=1)
    members, starts = [0], [0]
    for axis in "zyxc":
        steps = [i * strides[axis] for i in range(sizes[axis])]
        if axis in axes:
            members = [m + i for m in members for i in steps]
        else:
            starts = [m + i for m in starts for i in steps]
    groups = [[start + m for m in members] for start in starts]
    return lax.all_to_all(
        array, ("dp", "tile"), split_axis=0, concat_axis=0, axis_index_groups=groups, tiled=True
    )


def on_device(embeddings, cluster_ids, padding):
    rows, features = embeddings.shape
    tile = lax.axis_index("tile")
    chip, core = tile // 2, tile % 2
    groups = jnp.stack(
        [
            tile,
            2 * chip + 1 - core,
            2 * ((chip + 3) % 4) + jnp.where(chip > 0, 1 - core, core),
            2 * ((chip + 1) % 4) + jnp.where(chip == 3, 1 - core, core),
        ]
    ).astype(jnp.int32)
    packed, place = pack(tile, cluster_ids, padding, embeddings)
    packed = packed.reshape(OWNERS, PART, features + 128)
    received = lax.all_to_all(packed, "dp", split_axis=0, concat_axis=0, tiled=True)
    received = received.reshape(ROWS, features + 128)
    a, tag = lax.optimization_barrier((received[:, :features], received[:, features:]))
    swap = [(2 * x + c, 2 * x + 1 - c) for x in range(4) for c in range(2)]
    backward = [
        (2 * ((x + 1) % 4) + c, 2 * x + (c ^ NEXT_CROSSED[x])) for x in range(4) for c in range(2)
    ]
    forward = [
        (2 * ((x + 3) % 4) + c, 2 * x + (c ^ PREVIOUS_CROSSED[x]))
        for x in range(4)
        for c in range(2)
    ]
    p = lax.ppermute(a, "tile", forward)
    n = lax.ppermute(a, "tile", backward)
    b = lax.ppermute(a, "tile", swap)
    marks_shape = jax.ShapeDtypeStruct((4 * ROWS, 128), jnp.bfloat16)
    best, marks = scores(own_kernel, groups, tag, a, out_shape=(PARTIAL, marks_shape))
    best = scores(previous_kernel, groups, marks, best, a, p)
    best = scores(last_kernel, groups, marks, best, a, b, p, n)
    best = jnp.broadcast_to(best.reshape(8, 1, 4, 128), (8, 2, 4, 128)).reshape(16, 4, 128)
    best = exchange(best, "zc").reshape(8, 2, 4, 128)
    best = jnp.max(best, axis=1)
    best = jnp.concatenate([best[:, :, :CAPACITY], best[:, :, CAPACITY:]], axis=1)
    best = best.transpose(1, 0, 2)
    best = jnp.concatenate([best[:, :4], best[:, 4:]], axis=2)
    best = jnp.broadcast_to(best[:, None], (8, 4, 4, 128)).reshape(32, 4, 128)
    best = exchange(best, "yx").reshape(8, 4, 4, 128)
    return pick(place, best).reshape(rows)


def solution(mesh):
    in_specs = (P("dp", None), P("dp"), P("dp"))
    out_specs = P("dp")
    return jax.shard_map(
        on_device, mesh=mesh, in_specs=in_specs, out_specs=out_specs, check_vma=False
    )
```

```python
import jax
import jax.numpy as jnp
from jax import lax
from jax.experimental import pallas as pl
from jax.experimental.pallas import tpu as pltpu
from jax.sharding import PartitionSpec as P

OWNERS = 64
CAPACITY = 64
TILES = 8
PART = CAPACITY // TILES
ROWS = OWNERS * PART
TAG = 2.0
PLACE_FLOPS = 2_000_000_000
VMEM = 16 * 1024 * 1024


def iota(shape, dim):
    return lax.broadcasted_iota(jnp.int32, shape, dim)


def nt_dot(a, b):
    return lax.dot_general(a, b, (((1,), (1,)), ((), ())), preferred_element_type=jnp.float32)


def one_hot(flags):
    return jnp.where(flags, jnp.float32(1), jnp.float32(0)).astype(jnp.bfloat16)


def place_kernel(tile_ref, labels_ref, place_ref, wanted_ref, tag_ref, tags):
    rows = labels_ref.shape[1]
    width = 256
    labels = labels_ref[...]
    owner = jnp.where(labels >= 0, labels & (OWNERS - 1), -1)
    member_hot = one_hot(owner == iota((OWNERS, rows), 0))
    strictly_before = one_hot(iota((width, width), 0) < iota((width, width), 1))
    carry = jnp.zeros((OWNERS, 1), jnp.float32)
    slots = []
    for start in range(0, rows, width):
        block = member_hot[:, start : start + width]
        rank = carry + jnp.dot(block, strictly_before, preferred_element_type=jnp.float32)
        block = block.astype(jnp.float32)
        slots.append(jnp.sum(block * rank, axis=0, keepdims=True))
        carry = carry + jnp.sum(block, axis=1, keepdims=True)
    slot = jnp.concatenate(slots, axis=1).astype(jnp.int32)
    place_ref[...] = jnp.where(owner >= 0, owner * CAPACITY + slot, -1)
    part = slot >> 3
    local = slot & (PART - 1)
    wanted_ref[...] = jnp.where((owner >= 0) & (part == tile_ref[0]), owner * PART + local, -1)
    cluster = jnp.where(owner >= 0, (labels >> 6) + 1, 0).astype(jnp.float32)
    here = local * TILES + part == iota((CAPACITY, rows), 0)
    slot_cluster = jnp.where(here, cluster, 0.0).astype(jnp.bfloat16)
    by_owner = nt_dot(member_hot, slot_cluster)
    tags[...] = jnp.zeros(tags.shape, jnp.float32)
    for i in range(PART):
        tags[:, i, :TILES] = by_owner[:, i * TILES : (i + 1) * TILES]
    tag_ref[...] = tags[...].reshape(ROWS, 128).astype(jnp.bfloat16)


def pack_kernel(wanted_ref, tag_ref, emb_ref, unit_ref):
    rows, features = emb_ref.shape
    pick = one_hot(iota((ROWS, rows), 0) == wanted_ref[...])
    total = jnp.dot(pick, emb_ref[...], preferred_element_type=jnp.float32)
    scale = lax.rsqrt(jnp.sum(total * total, axis=1, keepdims=True) + 1e-06)
    unit_ref[:, :features] = (total * scale).astype(jnp.bfloat16)
    unit_ref[:, features:] = tag_ref[...]


def marks_of(tag, group):
    take = one_hot((iota((128, 128), 0) == group) & (iota((128, 128), 1) < 4))
    cluster = jnp.dot(tag, take, preferred_element_type=jnp.float32)
    marked = cluster == (iota(tag.shape, 1) + 1).astype(jnp.float32)
    return jnp.where(marked, TAG, 0.0).astype(jnp.bfloat16)


def spread(best, group):
    row, lane = iota((ROWS, 128), 0), iota((ROWS, 128), 1)
    value = jnp.maximum(best - TAG * TAG, -1.0)
    here = lane == group * PART + (row & 7) + ((row >> 5) & 1) * CAPACITY
    placed = jnp.where(here, value, -2.0).reshape(8, 2, 4, PART, 128)
    return jnp.max(jnp.max(placed, axis=1), axis=2).reshape(32, 128)


def row_best(scores):
    return jnp.max(scores, axis=1, keepdims=True)


def column_best(scores):
    best = jnp.max(scores.reshape(scores.shape[0] // 8, 8, ROWS), axis=0)
    best = jnp.max(best, axis=0, keepdims=True)
    return jnp.broadcast_to(best, (128, ROWS)).T[:, :1]


def own_kernel(groups_ref, tag_ref, a_ref, out_ref, marks_ref):
    tag = tag_ref[...]
    for j in range(5):
        marks_ref[j * ROWS : (j + 1) * ROWS, :] = marks_of(tag, groups_ref[j])
    marks_a = marks_ref[:ROWS, :]
    a = a_ref[...]
    same = nt_dot(a, a) + nt_dot(marks_a, marks_a)
    same = jnp.where(iota((ROWS, ROWS), 0) == iota((ROWS, ROWS), 1), -2.0, same)
    out_ref[...] = spread(row_best(same), groups_ref[0])


def marks(marks_ref, j):
    return marks_ref[j * ROWS : (j + 1) * ROWS, :]


def with_marks(marks_ref, x, i, y, j):
    return nt_dot(x, y) + nt_dot(marks(marks_ref, i), marks(marks_ref, j))


def first_kernel(groups_ref, marks_ref, best_ref, a_ref, f_ref, b_ref, out_ref):
    a = a_ref[...]
    a_f = with_marks(marks_ref, a, 0, f_ref[...], 2)
    a_b = with_marks(marks_ref, a, 0, b_ref[...], 1)
    best = jnp.maximum(best_ref[...], spread(row_best(jnp.maximum(a_f, a_b)), groups_ref[0]))
    out_ref[...] = jnp.maximum(best, spread(column_best(a_f), groups_ref[2]))


def last_kernel(groups_ref, marks_ref, best_ref, a_ref, b_ref, f_ref, q_ref, s_ref, out_ref):
    f, q, s = f_ref[...], q_ref[...], s_ref[...]
    b_s = with_marks(marks_ref, b_ref[...], 1, s, 3)
    f_s = with_marks(marks_ref, f, 2, s, 3)
    a_q = with_marks(marks_ref, a_ref[...], 0, q, 4)
    f_q = with_marks(marks_ref, f, 2, q, 4)
    best = jnp.maximum(best_ref[...], spread(row_best(a_q), groups_ref[0]))
    best = jnp.maximum(best, spread(row_best(b_s), groups_ref[1]))
    out_ref[...] = jnp.maximum(best, spread(row_best(jnp.maximum(f_s, f_q)), groups_ref[2]))


def pick_kernel(place_ref, best_ref, out_ref):
    place = place_ref[...]
    rows = place.shape[1]
    owner = place >> 6
    z, y = owner >> 3, owner & 7
    owner_hot = one_hot(((z >> 2) << 5) + (y << 2) + (z & 3) == iota((OWNERS, rows), 0))
    best = jnp.max(best_ref[...], axis=1).reshape(32, 128).T
    best = jnp.concatenate([best[:CAPACITY], best[CAPACITY:]], axis=1)
    high = best.astype(jnp.bfloat16)
    rest = best - high.astype(jnp.float32)
    middle = rest.astype(jnp.bfloat16)
    low = (rest - middle.astype(jnp.float32)).astype(jnp.bfloat16)
    by_slot = (
        jnp.dot(high, owner_hot, preferred_element_type=jnp.float32)
        + jnp.dot(middle, owner_hot, preferred_element_type=jnp.float32)
        + jnp.dot(low, owner_hot, preferred_element_type=jnp.float32)
    )
    here = (place & (CAPACITY - 1)) == iota((CAPACITY, rows), 0)
    picked = jnp.sum(jnp.where(here, by_slot, 0.0), axis=0, keepdims=True)
    out_ref[...] = jnp.where(place >= 0, picked, -1.0)


def call(kernel, out_shape, in_specs, flops=0, scratch=()):
    return pl.pallas_call(
        kernel,
        out_shape=out_shape,
        in_specs=in_specs,
        scratch_shapes=list(scratch),
        compiler_params=pltpu.CompilerParams(vmem_limit_bytes=VMEM),
        cost_estimate=pl.CostEstimate(flops=flops, bytes_accessed=1 << 20, transcendentals=0),
    )


VMEM_SPEC = pl.BlockSpec(memory_space=pltpu.VMEM)
SMEM_SPEC = pl.BlockSpec(memory_space=pltpu.SMEM)
PARTIAL = jax.ShapeDtypeStruct((32, 128), jnp.float32)


def pack(tile, cluster_ids, padding, embeddings):
    rows, features = embeddings.shape
    labels = jnp.where(padding == 0, cluster_ids, -1).reshape(1, rows)
    row = jax.ShapeDtypeStruct((1, rows), jnp.int32)
    place, wanted, tag = call(
        place_kernel,
        (row, row, jax.ShapeDtypeStruct((ROWS, 128), jnp.bfloat16)),
        [SMEM_SPEC, VMEM_SPEC],
        flops=PLACE_FLOPS,
        scratch=[pltpu.VMEM((OWNERS, PART, 128), jnp.float32)],
    )(tile.reshape(1), labels)
    packed = call(
        pack_kernel,
        jax.ShapeDtypeStruct((ROWS, features + 128), jnp.bfloat16),
        [VMEM_SPEC] * 3,
        flops=2 * ROWS * rows * features,
    )(wanted, tag, embeddings)
    return packed, place


def scores(kernel, groups, *arrays, out_shape=PARTIAL):
    flops = 4 * ROWS * ROWS * arrays[-1].shape[1]
    specs = [SMEM_SPEC] + [VMEM_SPEC] * len(arrays)
    return call(kernel, out_shape, specs, flops)(groups, *arrays)


def pick(place, best):
    out_shape = jax.ShapeDtypeStruct(place.shape, jnp.float32)
    return call(pick_kernel, out_shape, [VMEM_SPEC] * 2)(place, best)


def exchange(array, axes):
    sizes = dict(z=8, y=8, x=4, c=2)
    strides = dict(z=64, y=8, x=2, c=1)
    members, starts = [0], [0]
    for axis in "zyxc":
        steps = [i * strides[axis] for i in range(sizes[axis])]
        if axis in axes:
            members = [m + i for m in members for i in steps]
        else:
            starts = [m + i for m in starts for i in steps]
    groups = [[start + m for m in members] for start in starts]
    return lax.all_to_all(
        array, ("dp", "tile"), split_axis=0, concat_axis=0, axis_index_groups=groups, tiled=True
    )


def on_device(embeddings, cluster_ids, padding):
    rows, features = embeddings.shape
    tile = lax.axis_index("tile")
    chip, core = tile // 2, tile % 2
    before, after = (chip + 3) % 4, (chip + 1) % 4
    groups = jnp.stack(
        [
            tile,
            2 * chip + 1 - core,
            2 * jnp.where(core == 0, before, after) + core,
            2 * jnp.where(core == 0, after, before) + core,
            2 * jnp.where(core == 0, after, before) + 1 - core,
        ]
    ).astype(jnp.int32)
    packed, place = pack(tile, cluster_ids, padding, embeddings)
    packed = packed.reshape(OWNERS, PART, features + 128)
    received = lax.all_to_all(packed, "dp", split_axis=0, concat_axis=0, tiled=True)
    received = received.reshape(ROWS, features + 128)
    a, tag = lax.optimization_barrier((received[:, :features], received[:, features:]))
    swap = [(2 * x + c, 2 * x + 1 - c) for x in range(4) for c in range(2)]
    up = [[(2 * x + c, 2 * ((x + 1) % 4) + c) for x in range(4)] for c in range(2)]
    down = [[(2 * x + c, 2 * ((x + 3) % 4) + c) for x in range(4)] for c in range(2)]
    first = lax.ppermute(a, "tile", up[0] + down[1])
    b = lax.ppermute(a, "tile", swap)
    marks_shape = jax.ShapeDtypeStruct((5 * ROWS, 128), jnp.bfloat16)
    best, marks = scores(own_kernel, groups, tag, a, out_shape=(PARTIAL, marks_shape))
    later, best = lax.optimization_barrier((a, best))
    second = lax.ppermute(later, "tile", down[0] + up[1])
    crossed = lax.ppermute(first, "tile", swap)
    best = scores(first_kernel, groups, marks, best, a, first, b)
    best = scores(last_kernel, groups, marks, best, a, b, first, crossed, second)
    best = jnp.broadcast_to(best.reshape(8, 1, 4, 128), (8, 2, 4, 128)).reshape(16, 4, 128)
    best = exchange(best, "zc").reshape(8, 2, 4, 128)
    best = jnp.max(best, axis=1)
    best = jnp.concatenate([best[:, :, :CAPACITY], best[:, :, CAPACITY:]], axis=1)
    best = best.transpose(1, 0, 2)
    best = jnp.concatenate([best[:, :4], best[:, 4:]], axis=2)
    best = jnp.broadcast_to(best[:, None], (8, 4, 4, 128)).reshape(32, 4, 128)
    best = exchange(best, "yx").reshape(8, 4, 4, 128)
    return pick(place, best).reshape(rows)


def solution(mesh):
    in_specs = (P("dp", None), P("dp"), P("dp"))
    out_specs = P("dp")
    return jax.shard_map(
        on_device, mesh=mesh, in_specs=in_specs, out_specs=out_specs, check_vma=False
    )
```

```python
import jax
import jax.numpy as jnp
from jax import lax
from jax.experimental import pallas as pl
from jax.experimental.pallas import tpu as pltpu
from jax.sharding import PartitionSpec as P

OWNERS = 64
CAPACITY = 64
TILES = 8
PART = CAPACITY // TILES
ROWS = OWNERS * PART
PARTS = 5
PLACE_FLOPS = 2_000_000_000
VMEM = 16 * 1024 * 1024


def iota(shape, dim):
    return lax.broadcasted_iota(jnp.int32, shape, dim)


def nt_dot(a, b):
    return lax.dot_general(a, b, (((1,), (1,)), ((), ())), preferred_element_type=jnp.float32)


def one_hot(flags):
    return jnp.where(flags, jnp.float32(1), jnp.float32(0)).astype(jnp.bfloat16)


def place_kernel(tile_ref, labels_ref, place_ref, wanted_ref, tag_ref, tags):
    rows = labels_ref.shape[1]
    width = 256
    labels = labels_ref[...]
    owner = jnp.where(labels >= 0, labels & (OWNERS - 1), -1)
    member_hot = one_hot(owner == iota((OWNERS, rows), 0))
    strictly_before = one_hot(iota((width, width), 0) < iota((width, width), 1))
    carry = jnp.zeros((OWNERS, 1), jnp.float32)
    slots = []
    for start in range(0, rows, width):
        block = member_hot[:, start : start + width]
        rank = carry + jnp.dot(block, strictly_before, preferred_element_type=jnp.float32)
        block = block.astype(jnp.float32)
        slots.append(jnp.sum(block * rank, axis=0, keepdims=True))
        carry = carry + jnp.sum(block, axis=1, keepdims=True)
    slot = jnp.concatenate(slots, axis=1).astype(jnp.int32)
    place_ref[...] = jnp.where(owner >= 0, owner * CAPACITY + slot, -1)
    part = slot >> 3
    local = slot & (PART - 1)
    wanted_ref[...] = jnp.where((owner >= 0) & (part == tile_ref[0]), owner * PART + local, -1)
    cluster = jnp.where(owner >= 0, (labels >> 6) + 1, 0).astype(jnp.float32)
    here = local * TILES + part == iota((CAPACITY, rows), 0)
    slot_cluster = jnp.where(here, cluster, 0.0).astype(jnp.bfloat16)
    by_owner = nt_dot(member_hot, slot_cluster)
    tags[...] = jnp.zeros(tags.shape, jnp.float32)
    for i in range(PART):
        tags[:, i, :TILES] = by_owner[:, i * TILES : (i + 1) * TILES]
    tag_ref[...] = tags[...].reshape(ROWS, 128).astype(jnp.bfloat16)


def pack_kernel(wanted_ref, tag_ref, emb_ref, unit_ref):
    rows, features = emb_ref.shape
    pick = one_hot(iota((ROWS, rows), 0) == wanted_ref[...])
    total = jnp.dot(pick, emb_ref[...], preferred_element_type=jnp.float32)
    scale = lax.rsqrt(jnp.sum(total * total, axis=1, keepdims=True) + 1e-06)
    unit_ref[:, :features] = (total * scale).astype(jnp.bfloat16)
    unit_ref[:, features:] = tag_ref[...]


def clusters_of(tag, group):
    take = one_hot(iota((128, 128), 0) == group)
    return jnp.dot(tag, take, preferred_element_type=jnp.float32)


def spread(*bests):
    row, lane = iota((ROWS, 128), 0), iota((ROWS, 128), 1)
    slot = lane - (row & 7) - ((row >> 5) & 1) * CAPACITY
    placed = jnp.full((ROWS, 128), -2.0, jnp.float32)
    for best, group in bests:
        placed = jnp.where(slot == group * PART, jnp.maximum(best, -1.0), placed)
    placed = placed.reshape(8, 2, 4, PART, 128)
    return jnp.max(jnp.max(placed, axis=1), axis=2).reshape(32, 128)


def row_best(scores):
    return jnp.max(scores, axis=1, keepdims=True)


def column_best(scores):
    best = jnp.max(scores.reshape(scores.shape[0] // 8, 8, ROWS), axis=0)
    best = jnp.max(best, axis=0, keepdims=True)
    return jnp.broadcast_to(best, (128, ROWS)).T[:, :1]


def same_cluster(rows_ref, i, columns_ref, j):
    rows = rows_ref[i * ROWS : (i + 1) * ROWS, :]
    return jnp.concatenate([rows] * (ROWS // 128), axis=1) == columns_ref[j * 8 : j * 8 + 1, :]


def masked_scores(rows_ref, columns_ref, x, i, y, j):
    return jnp.where(same_cluster(rows_ref, i, columns_ref, j), nt_dot(x, y), -1.0)


def own_kernel(groups_ref, tag_ref, a_ref, out_ref, rows_ref, columns_ref):
    tag = tag_ref[...]
    for j in range(PARTS):
        clusters = clusters_of(tag, groups_ref[j])
        rows_ref[j * ROWS : (j + 1) * ROWS, :] = jnp.where(clusters == 0.0, -1.0, clusters)
        columns_ref[j * 8 : (j + 1) * 8, :] = clusters.T[:8, :]
    a = a_ref[...]
    scores = masked_scores(rows_ref, columns_ref, a, 0, a, 0)
    scores = jnp.where(iota((ROWS, ROWS), 0) == iota((ROWS, ROWS), 1), -1.0, scores)
    out_ref[...] = spread((row_best(scores), groups_ref[0]))


def first_kernel(groups_ref, rows_ref, columns_ref, best_ref, a_ref, f_ref, b_ref, out_ref):
    a = a_ref[...]
    a_f = masked_scores(rows_ref, columns_ref, a, 0, f_ref[...], 2)
    a_b = masked_scores(rows_ref, columns_ref, a, 0, b_ref[...], 1)
    best = spread(
        (row_best(jnp.maximum(a_f, a_b)), groups_ref[0]), (column_best(a_f), groups_ref[2])
    )
    out_ref[...] = jnp.maximum(best_ref[...], best)


def last_kernel(groups_ref, rows_ref, columns_ref, best_ref, a_ref, b_ref, f_ref, q_ref, s_ref, out_ref):
    f, q, s = f_ref[...], q_ref[...], s_ref[...]
    b_s = masked_scores(rows_ref, columns_ref, b_ref[...], 1, s, 3)
    f_s = masked_scores(rows_ref, columns_ref, f, 2, s, 3)
    a_q = masked_scores(rows_ref, columns_ref, a_ref[...], 0, q, 4)
    f_q = masked_scores(rows_ref, columns_ref, f, 2, q, 4)
    best = spread(
        (row_best(a_q), groups_ref[0]),
        (row_best(b_s), groups_ref[1]),
        (row_best(jnp.maximum(f_s, f_q)), groups_ref[2]),
    )
    out_ref[...] = jnp.maximum(best_ref[...], best)


def pick_kernel(place_ref, best_ref, out_ref):
    place = place_ref[...]
    rows = place.shape[1]
    owner = place >> 6
    z, y = owner >> 3, owner & 7
    owner_hot = one_hot(((z >> 2) << 5) + (y << 2) + (z & 3) == iota((OWNERS, rows), 0))
    best = jnp.max(best_ref[...], axis=1).reshape(32, 128).T
    best = jnp.concatenate([best[:CAPACITY], best[CAPACITY:]], axis=1)
    high = best.astype(jnp.bfloat16)
    rest = best - high.astype(jnp.float32)
    middle = rest.astype(jnp.bfloat16)
    low = (rest - middle.astype(jnp.float32)).astype(jnp.bfloat16)
    by_slot = (
        jnp.dot(high, owner_hot, preferred_element_type=jnp.float32)
        + jnp.dot(middle, owner_hot, preferred_element_type=jnp.float32)
        + jnp.dot(low, owner_hot, preferred_element_type=jnp.float32)
    )
    here = (place & (CAPACITY - 1)) == iota((CAPACITY, rows), 0)
    picked = jnp.sum(jnp.where(here, by_slot, 0.0), axis=0, keepdims=True)
    out_ref[...] = jnp.where(place >= 0, picked, -1.0)


def call(kernel, out_shape, in_specs, flops=0, scratch=()):
    return pl.pallas_call(
        kernel,
        out_shape=out_shape,
        in_specs=in_specs,
        scratch_shapes=list(scratch),
        compiler_params=pltpu.CompilerParams(vmem_limit_bytes=VMEM),
        cost_estimate=pl.CostEstimate(flops=flops, bytes_accessed=1 << 20, transcendentals=0),
    )


VMEM_SPEC = pl.BlockSpec(memory_space=pltpu.VMEM)
SMEM_SPEC = pl.BlockSpec(memory_space=pltpu.SMEM)
PARTIAL = jax.ShapeDtypeStruct((32, 128), jnp.float32)


def pack(tile, cluster_ids, padding, embeddings):
    rows, features = embeddings.shape
    labels = jnp.where(padding == 0, cluster_ids, -1).reshape(1, rows)
    row = jax.ShapeDtypeStruct((1, rows), jnp.int32)
    place, wanted, tag = call(
        place_kernel,
        (row, row, jax.ShapeDtypeStruct((ROWS, 128), jnp.bfloat16)),
        [SMEM_SPEC, VMEM_SPEC],
        flops=PLACE_FLOPS,
        scratch=[pltpu.VMEM((OWNERS, PART, 128), jnp.float32)],
    )(tile.reshape(1), labels)
    packed = call(
        pack_kernel,
        jax.ShapeDtypeStruct((ROWS, features + 128), jnp.bfloat16),
        [VMEM_SPEC] * 3,
        flops=2 * ROWS * rows * features,
    )(wanted, tag, embeddings)
    return packed, place


def scores(kernel, groups, *arrays, out_shape=PARTIAL):
    flops = 4 * ROWS * ROWS * arrays[-1].shape[1]
    specs = [SMEM_SPEC] + [VMEM_SPEC] * len(arrays)
    return call(kernel, out_shape, specs, flops)(groups, *arrays)


def pick(place, best):
    out_shape = jax.ShapeDtypeStruct(place.shape, jnp.float32)
    return call(pick_kernel, out_shape, [VMEM_SPEC] * 2)(place, best)


def exchange(array, axes):
    sizes = dict(z=8, y=8, x=4, c=2)
    strides = dict(z=64, y=8, x=2, c=1)
    members, starts = [0], [0]
    for axis in "zyxc":
        steps = [i * strides[axis] for i in range(sizes[axis])]
        if axis in axes:
            members = [m + i for m in members for i in steps]
        else:
            starts = [m + i for m in starts for i in steps]
    groups = [[start + m for m in members] for start in starts]
    return lax.all_to_all(
        array, ("dp", "tile"), split_axis=0, concat_axis=0, axis_index_groups=groups, tiled=True
    )


def on_device(embeddings, cluster_ids, padding):
    rows, features = embeddings.shape
    tile = lax.axis_index("tile")
    chip, core = tile // 2, tile % 2
    before, after = (chip + 3) % 4, (chip + 1) % 4
    groups = jnp.stack(
        [
            tile,
            2 * chip + 1 - core,
            2 * jnp.where(core == 0, before, after) + core,
            2 * jnp.where(core == 0, after, before) + core,
            2 * jnp.where(core == 0, after, before) + 1 - core,
        ]
    ).astype(jnp.int32)
    packed, place = pack(tile, cluster_ids, padding, embeddings)
    packed = packed.reshape(OWNERS, PART, features + 128)
    received = lax.all_to_all(packed, "dp", split_axis=0, concat_axis=0, tiled=True)
    received = received.reshape(ROWS, features + 128)
    a, tag = lax.optimization_barrier((received[:, :features], received[:, features:]))
    swap = [(2 * x + c, 2 * x + 1 - c) for x in range(4) for c in range(2)]
    up = [[(2 * x + c, 2 * ((x + 1) % 4) + c) for x in range(4)] for c in range(2)]
    down = [[(2 * x + c, 2 * ((x + 3) % 4) + c) for x in range(4)] for c in range(2)]
    first = lax.ppermute(a, "tile", up[0] + down[1])
    b = lax.ppermute(a, "tile", swap)
    clusters = [
        jax.ShapeDtypeStruct((PARTS * ROWS, 128), jnp.float32),
        jax.ShapeDtypeStruct((PARTS * 8, ROWS), jnp.float32),
    ]
    best, *clusters = scores(own_kernel, groups, tag, a, out_shape=[PARTIAL] + clusters)
    later, best = lax.optimization_barrier((a, best))
    second = lax.ppermute(later, "tile", down[0] + up[1])
    crossed = lax.ppermute(first, "tile", swap)
    best = scores(first_kernel, groups, *clusters, best, a, first, b)
    best = scores(last_kernel, groups, *clusters, best, a, b, first, crossed, second)
    best = jnp.broadcast_to(best.reshape(8, 1, 4, 128), (8, 2, 4, 128)).reshape(16, 4, 128)
    best = exchange(best, "zc").reshape(8, 2, 4, 128)
    best = jnp.max(best, axis=1)
    best = jnp.concatenate([best[:, :, :CAPACITY], best[:, :, CAPACITY:]], axis=1)
    best = best.transpose(1, 0, 2)
    best = jnp.concatenate([best[:, :4], best[:, 4:]], axis=2)
    best = jnp.broadcast_to(best[:, None], (8, 4, 4, 128)).reshape(32, 4, 128)
    best = exchange(best, "yx").reshape(8, 4, 4, 128)
    return pick(place, best).reshape(rows)


def solution(mesh):
    in_specs = (P("dp", None), P("dp"), P("dp"))
    out_specs = P("dp")
    return jax.shard_map(
        on_device, mesh=mesh, in_specs=in_specs, out_specs=out_specs, check_vma=False
    )
```

```python
import jax
import jax.numpy as jnp
from jax import lax
from jax.experimental import pallas as pl
from jax.experimental.pallas import tpu as pltpu
from jax.sharding import PartitionSpec as P

OWNERS = 64
CAPACITY = 64
TILES = 8
PART = CAPACITY // TILES
ROWS = OWNERS * PART
PARTS = 5
PLACE_FLOPS = 2_000_000_000
VMEM = 16 * 1024 * 1024


def iota(shape, dim):
    return lax.broadcasted_iota(jnp.int32, shape, dim)


def nt_dot(a, b):
    return lax.dot_general(a, b, (((1,), (1,)), ((), ())), preferred_element_type=jnp.float32)


def one_hot(flags):
    return jnp.where(flags, jnp.float32(1), jnp.float32(0)).astype(jnp.bfloat16)


def place_kernel(tile_ref, labels_ref, place_ref, wanted_ref, tag_ref, tags):
    rows = labels_ref.shape[1]
    width = 256
    labels = labels_ref[...]
    owner = jnp.where(labels >= 0, labels & (OWNERS - 1), -1)
    member_hot = one_hot(owner == iota((OWNERS, rows), 0))
    strictly_before = one_hot(iota((width, width), 0) < iota((width, width), 1))
    carry = jnp.zeros((OWNERS, 1), jnp.float32)
    slots = []
    for start in range(0, rows, width):
        block = member_hot[:, start : start + width]
        rank = carry + jnp.dot(block, strictly_before, preferred_element_type=jnp.float32)
        block = block.astype(jnp.float32)
        slots.append(jnp.sum(block * rank, axis=0, keepdims=True))
        carry = carry + jnp.sum(block, axis=1, keepdims=True)
    slot = jnp.concatenate(slots, axis=1).astype(jnp.int32)
    place_ref[...] = jnp.where(owner >= 0, owner * CAPACITY + slot, -1)
    part = slot >> 3
    local = slot & (PART - 1)
    wanted_ref[...] = jnp.where((owner >= 0) & (part == tile_ref[0]), owner * PART + local, -1)
    cluster = jnp.where(owner >= 0, (labels >> 6) + 1, 0).astype(jnp.float32)
    here = local * TILES + part == iota((CAPACITY, rows), 0)
    slot_cluster = jnp.where(here, cluster, 0.0).astype(jnp.bfloat16)
    by_owner = nt_dot(member_hot, slot_cluster)
    tags[...] = jnp.zeros(tags.shape, jnp.float32)
    for i in range(PART):
        tags[:, i, :TILES] = by_owner[:, i * TILES : (i + 1) * TILES]
    tag_ref[...] = tags[...].reshape(ROWS, 128).astype(jnp.bfloat16)


def pack_kernel(wanted_ref, tag_ref, emb_ref, unit_ref):
    rows, features = emb_ref.shape
    pick = one_hot(iota((ROWS, rows), 0) == wanted_ref[...])
    total = jnp.dot(pick, emb_ref[...], preferred_element_type=jnp.float32)
    scale = lax.rsqrt(jnp.sum(total * total, axis=1, keepdims=True) + 1e-06)
    unit_ref[:, :features] = (total * scale).astype(jnp.bfloat16)
    unit_ref[:, features:] = tag_ref[...]


def clusters_of(tag, group):
    take = one_hot(iota((128, 128), 0) == group)
    return jnp.dot(tag, take, preferred_element_type=jnp.float32)


def spread(*bests):
    row, lane = iota((ROWS, 128), 0), iota((ROWS, 128), 1)
    slot = lane - (row & 7) - ((row >> 5) & 1) * CAPACITY
    placed = jnp.full((ROWS, 128), -2.0, jnp.float32)
    for best, group in bests:
        placed = jnp.where(slot == group * PART, jnp.maximum(best, -1.0), placed)
    placed = placed.reshape(8, 2, 4, PART, 128)
    return jnp.max(jnp.max(placed, axis=1), axis=2).reshape(32, 128)


def row_best(scores):
    return jnp.max(scores, axis=1, keepdims=True)


def column_best(scores):
    best = jnp.max(scores.reshape(scores.shape[0] // 8, 8, ROWS), axis=0)
    best = jnp.max(best, axis=0, keepdims=True)
    return jnp.broadcast_to(best, (128, ROWS)).T[:, :1]


def same_cluster(rows_ref, i, columns_ref, j):
    rows = rows_ref[i * ROWS : (i + 1) * ROWS, :]
    return jnp.concatenate([rows] * (ROWS // 128), axis=1) == columns_ref[j * 8 : j * 8 + 1, :]


def masked_scores(rows_ref, columns_ref, x, i, y, j):
    return jnp.where(same_cluster(rows_ref, i, columns_ref, j), nt_dot(x, y), -1.0)


def own_kernel(groups_ref, tag_ref, a_ref, out_ref, rows_ref, columns_ref):
    tag = tag_ref[...]
    for j in range(PARTS):
        clusters = clusters_of(tag, groups_ref[j])
        rows_ref[j * ROWS : (j + 1) * ROWS, :] = jnp.where(clusters == 0.0, -1.0, clusters)
        columns_ref[j * 8 : (j + 1) * 8, :] = clusters.T[:8, :]
    a = a_ref[...]
    scores = masked_scores(rows_ref, columns_ref, a, 0, a, 0)
    scores = jnp.where(iota((ROWS, ROWS), 0) == iota((ROWS, ROWS), 1), -1.0, scores)
    out_ref[...] = spread((row_best(scores), groups_ref[0]))


def first_kernel(groups_ref, rows_ref, columns_ref, best_ref, a_ref, f_ref, b_ref, out_ref):
    a = a_ref[...]
    a_f = masked_scores(rows_ref, columns_ref, a, 0, f_ref[...], 2)
    a_b = masked_scores(rows_ref, columns_ref, a, 0, b_ref[...], 1)
    best = spread(
        (row_best(jnp.maximum(a_f, a_b)), groups_ref[0]), (column_best(a_f), groups_ref[2])
    )
    out_ref[...] = jnp.maximum(best_ref[...], best)


def last_kernel(groups_ref, rows_ref, columns_ref, best_ref, a_ref, b_ref, f_ref, q_ref, s_ref, out_ref):
    f, q, s = f_ref[...], q_ref[...], s_ref[...]
    b_s = masked_scores(rows_ref, columns_ref, b_ref[...], 1, s, 3)
    f_s = masked_scores(rows_ref, columns_ref, f, 2, s, 3)
    a_q = masked_scores(rows_ref, columns_ref, a_ref[...], 0, q, 4)
    f_q = masked_scores(rows_ref, columns_ref, f, 2, q, 4)
    best = spread(
        (row_best(a_q), groups_ref[0]),
        (row_best(b_s), groups_ref[1]),
        (row_best(jnp.maximum(f_s, f_q)), groups_ref[2]),
    )
    out_ref[...] = jnp.maximum(best_ref[...], best)


def pick_kernel(place_ref, best_ref, out_ref):
    place = place_ref[...]
    rows = place.shape[1]
    owner = place >> 6
    z, y = owner >> 3, owner & 7
    owner_hot = one_hot(((z >> 2) << 5) + (y << 2) + (z & 3) == iota((OWNERS, rows), 0))
    best = jnp.max(best_ref[...], axis=0).reshape(32, 128).T
    best = jnp.concatenate([best[:CAPACITY], best[CAPACITY:]], axis=1)
    high = best.astype(jnp.bfloat16)
    rest = best - high.astype(jnp.float32)
    middle = rest.astype(jnp.bfloat16)
    low = (rest - middle.astype(jnp.float32)).astype(jnp.bfloat16)
    by_slot = (
        jnp.dot(high, owner_hot, preferred_element_type=jnp.float32)
        + jnp.dot(middle, owner_hot, preferred_element_type=jnp.float32)
        + jnp.dot(low, owner_hot, preferred_element_type=jnp.float32)
    )
    here = (place & (CAPACITY - 1)) == iota((CAPACITY, rows), 0)
    picked = jnp.sum(jnp.where(here, by_slot, 0.0), axis=0, keepdims=True)
    out_ref[...] = jnp.where(place >= 0, picked, -1.0)


def call(kernel, out_shape, in_specs, flops=0, scratch=()):
    return pl.pallas_call(
        kernel,
        out_shape=out_shape,
        in_specs=in_specs,
        scratch_shapes=list(scratch),
        compiler_params=pltpu.CompilerParams(vmem_limit_bytes=VMEM),
        cost_estimate=pl.CostEstimate(flops=flops, bytes_accessed=1 << 20, transcendentals=0),
    )


VMEM_SPEC = pl.BlockSpec(memory_space=pltpu.VMEM)
SMEM_SPEC = pl.BlockSpec(memory_space=pltpu.SMEM)
PARTIAL = jax.ShapeDtypeStruct((32, 128), jnp.float32)


def pack(tile, cluster_ids, padding, embeddings):
    rows, features = embeddings.shape
    labels = jnp.where(padding == 0, cluster_ids, -1).reshape(1, rows)
    row = jax.ShapeDtypeStruct((1, rows), jnp.int32)
    place, wanted, tag = call(
        place_kernel,
        (row, row, jax.ShapeDtypeStruct((ROWS, 128), jnp.bfloat16)),
        [SMEM_SPEC, VMEM_SPEC],
        flops=PLACE_FLOPS,
        scratch=[pltpu.VMEM((OWNERS, PART, 128), jnp.float32)],
    )(tile.reshape(1), labels)
    packed = call(
        pack_kernel,
        jax.ShapeDtypeStruct((ROWS, features + 128), jnp.bfloat16),
        [VMEM_SPEC] * 3,
        flops=2 * ROWS * rows * features,
    )(wanted, tag, embeddings)
    return packed, place


def scores(kernel, groups, *arrays, out_shape=PARTIAL):
    flops = 4 * ROWS * ROWS * arrays[-1].shape[1]
    specs = [SMEM_SPEC] + [VMEM_SPEC] * len(arrays)
    return call(kernel, out_shape, specs, flops)(groups, *arrays)


def pick(place, best):
    out_shape = jax.ShapeDtypeStruct(place.shape, jnp.float32)
    return call(pick_kernel, out_shape, [VMEM_SPEC] * 2)(place, best)


def exchange(array, axes):
    sizes = dict(z=8, y=8, x=4, c=2)
    strides = dict(z=64, y=8, x=2, c=1)
    members, starts = [0], [0]
    for axis in axes:
        members = [m + i * strides[axis] for m in members for i in range(sizes[axis])]
    for axis in sizes:
        if axis not in axes:
            starts = [m + i * strides[axis] for m in starts for i in range(sizes[axis])]
    groups = [[start + m for m in members] for start in starts]
    return lax.all_to_all(
        array, ("dp", "tile"), split_axis=0, concat_axis=0, axis_index_groups=groups, tiled=True
    )


def on_device(embeddings, cluster_ids, padding):
    rows, features = embeddings.shape
    tile = lax.axis_index("tile")
    chip, core = tile // 2, tile % 2
    before, after = (chip + 3) % 4, (chip + 1) % 4
    groups = jnp.stack(
        [
            tile,
            2 * chip + 1 - core,
            2 * jnp.where(core == 0, before, after) + core,
            2 * jnp.where(core == 0, after, before) + core,
            2 * jnp.where(core == 0, after, before) + 1 - core,
        ]
    ).astype(jnp.int32)
    packed, place = pack(tile, cluster_ids, padding, embeddings)
    packed = packed.reshape(OWNERS, PART, features + 128)
    received = lax.all_to_all(packed, "dp", split_axis=0, concat_axis=0, tiled=True)
    received = received.reshape(ROWS, features + 128)
    a, tag = lax.optimization_barrier((received[:, :features], received[:, features:]))
    swap = [(2 * x + c, 2 * x + 1 - c) for x in range(4) for c in range(2)]
    up = [[(2 * x + c, 2 * ((x + 1) % 4) + c) for x in range(4)] for c in range(2)]
    down = [[(2 * x + c, 2 * ((x + 3) % 4) + c) for x in range(4)] for c in range(2)]
    first = lax.ppermute(a, "tile", up[0] + down[1])
    b = lax.ppermute(a, "tile", swap)
    clusters = [
        jax.ShapeDtypeStruct((PARTS * ROWS, 128), jnp.float32),
        jax.ShapeDtypeStruct((PARTS * 8, ROWS), jnp.float32),
    ]
    best, *clusters = scores(own_kernel, groups, tag, a, out_shape=[PARTIAL] + clusters)
    later, best = lax.optimization_barrier((a, best))
    second = lax.ppermute(later, "tile", down[0] + up[1])
    crossed = lax.ppermute(first, "tile", swap)
    best = scores(first_kernel, groups, *clusters, best, a, first, b)
    best = scores(last_kernel, groups, *clusters, best, a, b, first, crossed, second)
    best = jnp.broadcast_to(best.reshape(1, 8, 4, 128), (2, 8, 4, 128)).reshape(16, 4, 128)
    best = exchange(best, "cz").reshape(2, 8, 4, 128)
    best = jnp.max(best, axis=0)
    best = jnp.concatenate([best[:, :, :CAPACITY], best[:, :, CAPACITY:]], axis=1)
    best = best.transpose(1, 0, 2)
    best = jnp.concatenate([best[:, :4], best[:, 4:]], axis=2)
    best = jnp.broadcast_to(best[None], (4, 8, 4, 128)).reshape(32, 4, 128)
    best = exchange(best, "xy").reshape(4, 8, 4, 128)
    return pick(place, best).reshape(rows)


def solution(mesh):
    in_specs = (P("dp", None), P("dp"), P("dp"))
    out_specs = P("dp")
    return jax.shard_map(
        on_device, mesh=mesh, in_specs=in_specs, out_specs=out_specs, check_vma=False
    )
```

```python
import jax
import jax.numpy as jnp
from jax import lax
from jax.experimental import pallas as pl
from jax.experimental.pallas import tpu as pltpu
from jax.sharding import PartitionSpec as P

OWNERS = 64
CAPACITY = 64
TILES = 8
PART = CAPACITY // TILES
ROWS = OWNERS * PART
PARTS = 5
PLACE_FLOPS = 2_000_000_000
VMEM = 16 * 1024 * 1024


def iota(shape, dim):
    return lax.broadcasted_iota(jnp.int32, shape, dim)


def nt_dot(a, b):
    return lax.dot_general(a, b, (((1,), (1,)), ((), ())), preferred_element_type=jnp.float32)


def one_hot(flags):
    return jnp.where(flags, jnp.float32(1), jnp.float32(0)).astype(jnp.bfloat16)


def place_kernel(tile_ref, labels_ref, place_ref, wanted_ref, tag_ref, tags):
    rows = labels_ref.shape[1]
    width = 256
    labels = labels_ref[...]
    owner = jnp.where(labels >= 0, labels & (OWNERS - 1), -1)
    member_hot = one_hot(owner == iota((OWNERS, rows), 0))
    strictly_before = one_hot(iota((width, width), 0) < iota((width, width), 1))
    carry = jnp.zeros((OWNERS, 1), jnp.float32)
    slots = []
    for start in range(0, rows, width):
        block = member_hot[:, start : start + width]
        rank = carry + jnp.dot(block, strictly_before, preferred_element_type=jnp.float32)
        block = block.astype(jnp.float32)
        slots.append(jnp.sum(block * rank, axis=0, keepdims=True))
        carry = carry + jnp.sum(block, axis=1, keepdims=True)
    slot = jnp.concatenate(slots, axis=1).astype(jnp.int32)
    place_ref[...] = jnp.where(owner >= 0, owner * CAPACITY + slot, -1)
    part = slot >> 3
    local = slot & (PART - 1)
    wanted_ref[...] = jnp.where((owner >= 0) & (part == tile_ref[0]), owner * PART + local, -1)
    cluster = jnp.where(owner >= 0, (labels >> 6) + 1, 0).astype(jnp.float32)
    here = local * TILES + part == iota((CAPACITY, rows), 0)
    slot_cluster = jnp.where(here, cluster, 0.0).astype(jnp.bfloat16)
    by_owner = nt_dot(member_hot, slot_cluster)
    tags[...] = jnp.zeros(tags.shape, jnp.float32)
    for i in range(PART):
        tags[:, i, :TILES] = by_owner[:, i * TILES : (i + 1) * TILES]
    tag_ref[...] = tags[...].reshape(ROWS, 128).astype(jnp.bfloat16)


def pack_kernel(wanted_ref, tag_ref, emb_ref, unit_ref):
    rows, features = emb_ref.shape
    pick = one_hot(iota((ROWS, rows), 0) == wanted_ref[...])
    total = jnp.dot(pick, emb_ref[...], preferred_element_type=jnp.float32)
    scale = lax.rsqrt(jnp.sum(total * total, axis=1, keepdims=True) + 1e-06)
    unit_ref[:, :features] = (total * scale).astype(jnp.bfloat16)
    unit_ref[:, features:] = tag_ref[...]


def clusters_of(tag, group):
    take = one_hot(iota((128, 128), 0) == group)
    return jnp.dot(tag, take, preferred_element_type=jnp.float32)


def spread(*bests):
    row, lane = iota((ROWS, 128), 0), iota((ROWS, 128), 1)
    slot = lane - (row & 7) - ((row >> 5) & 1) * CAPACITY
    placed = jnp.full((ROWS, 128), -2.0, jnp.float32)
    for best, group in bests:
        placed = jnp.where(slot == group * PART, jnp.maximum(best, -1.0), placed)
    placed = placed.reshape(8, 2, 4, PART, 128)
    return jnp.max(jnp.max(placed, axis=1), axis=2).reshape(32, 128)


def row_best(scores):
    return jnp.max(scores, axis=1, keepdims=True)


def column_best(scores):
    best = jnp.max(scores.reshape(scores.shape[0] // 8, 8, ROWS), axis=0)
    best = jnp.max(best, axis=0, keepdims=True)
    return jnp.broadcast_to(best, (128, ROWS)).T[:, :1]


def same_cluster(rows_ref, i, columns_ref, j):
    rows = rows_ref[i * ROWS : (i + 1) * ROWS, :]
    return jnp.concatenate([rows] * (ROWS // 128), axis=1) == columns_ref[j * 8 : j * 8 + 1, :]


def masked_scores(rows_ref, columns_ref, x, i, y, j):
    return jnp.where(same_cluster(rows_ref, i, columns_ref, j), nt_dot(x, y), -1.0)


def own_kernel(groups_ref, tag_ref, a_ref, out_ref, rows_ref, columns_ref):
    tag = tag_ref[...]
    for j in range(PARTS):
        clusters = clusters_of(tag, groups_ref[j])
        rows_ref[j * ROWS : (j + 1) * ROWS, :] = jnp.where(clusters == 0.0, -1.0, clusters)
        columns_ref[j * 8 : (j + 1) * 8, :] = clusters.T[:8, :]
    a = a_ref[...]
    scores = masked_scores(rows_ref, columns_ref, a, 0, a, 0)
    scores = jnp.where(iota((ROWS, ROWS), 0) == iota((ROWS, ROWS), 1), -1.0, scores)
    out_ref[...] = spread((row_best(scores), groups_ref[0]))


def first_kernel(groups_ref, rows_ref, columns_ref, best_ref, a_ref, f_ref, b_ref, out_ref):
    a = a_ref[...]
    a_f = masked_scores(rows_ref, columns_ref, a, 0, f_ref[...], 2)
    a_b = masked_scores(rows_ref, columns_ref, a, 0, b_ref[...], 1)
    best = spread(
        (row_best(jnp.maximum(a_f, a_b)), groups_ref[0]), (column_best(a_f), groups_ref[2])
    )
    out_ref[...] = jnp.maximum(best_ref[...], best)


def last_kernel(groups_ref, rows_ref, columns_ref, best_ref, a_ref, b_ref, f_ref, q_ref, s_ref, out_ref):
    f, q, s = f_ref[...], q_ref[...], s_ref[...]
    with_s = nt_dot(jnp.concatenate([b_ref[...], f], axis=0), s)
    with_q = nt_dot(jnp.concatenate([a_ref[...], f], axis=0), q)
    b_s = jnp.where(same_cluster(rows_ref, 1, columns_ref, 3), with_s[:ROWS], -1.0)
    f_s = jnp.where(same_cluster(rows_ref, 2, columns_ref, 3), with_s[ROWS:], -1.0)
    a_q = jnp.where(same_cluster(rows_ref, 0, columns_ref, 4), with_q[:ROWS], -1.0)
    f_q = jnp.where(same_cluster(rows_ref, 2, columns_ref, 4), with_q[ROWS:], -1.0)
    best = spread(
        (row_best(a_q), groups_ref[0]),
        (row_best(b_s), groups_ref[1]),
        (row_best(jnp.maximum(f_s, f_q)), groups_ref[2]),
    )
    out_ref[...] = jnp.maximum(best_ref[...], best)


def pick_kernel(place_ref, best_ref, out_ref):
    place = place_ref[...]
    rows = place.shape[1]
    owner = place >> 6
    z, y = owner >> 3, owner & 7
    owner_hot = one_hot(((z >> 2) << 5) + (y << 2) + (z & 3) == iota((OWNERS, rows), 0))
    best = jnp.max(best_ref[...], axis=0).reshape(32, 128).T
    best = jnp.concatenate([best[:CAPACITY], best[CAPACITY:]], axis=1)
    high = best.astype(jnp.bfloat16)
    rest = best - high.astype(jnp.float32)
    middle = rest.astype(jnp.bfloat16)
    low = (rest - middle.astype(jnp.float32)).astype(jnp.bfloat16)
    by_slot = (
        jnp.dot(high, owner_hot, preferred_element_type=jnp.float32)
        + jnp.dot(middle, owner_hot, preferred_element_type=jnp.float32)
        + jnp.dot(low, owner_hot, preferred_element_type=jnp.float32)
    )
    here = (place & (CAPACITY - 1)) == iota((CAPACITY, rows), 0)
    picked = jnp.sum(jnp.where(here, by_slot, 0.0), axis=0, keepdims=True)
    out_ref[...] = jnp.where(place >= 0, picked, -1.0)


def call(kernel, out_shape, in_specs, flops=0, scratch=()):
    return pl.pallas_call(
        kernel,
        out_shape=out_shape,
        in_specs=in_specs,
        scratch_shapes=list(scratch),
        compiler_params=pltpu.CompilerParams(vmem_limit_bytes=VMEM),
        cost_estimate=pl.CostEstimate(flops=flops, bytes_accessed=1 << 20, transcendentals=0),
    )


VMEM_SPEC = pl.BlockSpec(memory_space=pltpu.VMEM)
SMEM_SPEC = pl.BlockSpec(memory_space=pltpu.SMEM)
PARTIAL = jax.ShapeDtypeStruct((32, 128), jnp.float32)


def pack(tile, cluster_ids, padding, embeddings):
    rows, features = embeddings.shape
    labels = jnp.where(padding == 0, cluster_ids, -1).reshape(1, rows)
    row = jax.ShapeDtypeStruct((1, rows), jnp.int32)
    place, wanted, tag = call(
        place_kernel,
        (row, row, jax.ShapeDtypeStruct((ROWS, 128), jnp.bfloat16)),
        [SMEM_SPEC, VMEM_SPEC],
        flops=PLACE_FLOPS,
        scratch=[pltpu.VMEM((OWNERS, PART, 128), jnp.float32)],
    )(tile.reshape(1), labels)
    packed = call(
        pack_kernel,
        jax.ShapeDtypeStruct((ROWS, features + 128), jnp.bfloat16),
        [VMEM_SPEC] * 3,
        flops=2 * ROWS * rows * features,
    )(wanted, tag, embeddings)
    return packed, place


def scores(kernel, groups, *arrays, out_shape=PARTIAL):
    flops = 4 * ROWS * ROWS * arrays[-1].shape[1]
    specs = [SMEM_SPEC] + [VMEM_SPEC] * len(arrays)
    return call(kernel, out_shape, specs, flops)(groups, *arrays)


def pick(place, best):
    out_shape = jax.ShapeDtypeStruct(place.shape, jnp.float32)
    return call(pick_kernel, out_shape, [VMEM_SPEC] * 2)(place, best)


def exchange(array, axes):
    sizes = dict(z=8, y=8, x=4, c=2)
    strides = dict(z=64, y=8, x=2, c=1)
    members, starts = [0], [0]
    for axis in axes:
        members = [m + i * strides[axis] for m in members for i in range(sizes[axis])]
    for axis in sizes:
        if axis not in axes:
            starts = [m + i * strides[axis] for m in starts for i in range(sizes[axis])]
    groups = [[start + m for m in members] for start in starts]
    return lax.all_to_all(
        array, ("dp", "tile"), split_axis=0, concat_axis=0, axis_index_groups=groups, tiled=True
    )


def on_device(embeddings, cluster_ids, padding):
    rows, features = embeddings.shape
    tile = lax.axis_index("tile")
    chip, core = tile // 2, tile % 2
    before, after = (chip + 3) % 4, (chip + 1) % 4
    groups = jnp.stack(
        [
            tile,
            2 * chip + 1 - core,
            2 * jnp.where(core == 0, before, after) + core,
            2 * jnp.where(core == 0, after, before) + core,
            2 * jnp.where(core == 0, after, before) + 1 - core,
        ]
    ).astype(jnp.int32)
    packed, place = pack(tile, cluster_ids, padding, embeddings)
    packed = packed.reshape(OWNERS, PART, features + 128)
    received = lax.all_to_all(packed, "dp", split_axis=0, concat_axis=0, tiled=True)
    received = received.reshape(ROWS, features + 128)
    a, tag = lax.optimization_barrier((received[:, :features], received[:, features:]))
    swap = [(2 * x + c, 2 * x + 1 - c) for x in range(4) for c in range(2)]
    up = [[(2 * x + c, 2 * ((x + 1) % 4) + c) for x in range(4)] for c in range(2)]
    down = [[(2 * x + c, 2 * ((x + 3) % 4) + c) for x in range(4)] for c in range(2)]
    first = lax.ppermute(a, "tile", up[0] + down[1])
    b = lax.ppermute(a, "tile", swap)
    clusters = [
        jax.ShapeDtypeStruct((PARTS * ROWS, 128), jnp.float32),
        jax.ShapeDtypeStruct((PARTS * 8, ROWS), jnp.float32),
    ]
    best, *clusters = scores(own_kernel, groups, tag, a, out_shape=[PARTIAL] + clusters)
    later, best = lax.optimization_barrier((a, best))
    second = lax.ppermute(later, "tile", down[0] + up[1])
    crossed = lax.ppermute(first, "tile", swap)
    best = scores(first_kernel, groups, *clusters, best, a, first, b)
    best = scores(last_kernel, groups, *clusters, best, a, b, first, crossed, second)
    best = jnp.broadcast_to(best.reshape(1, 8, 4, 128), (2, 8, 4, 128)).reshape(16, 4, 128)
    best = exchange(best, "cz").reshape(2, 8, 4, 128)
    best = jnp.max(best, axis=0)
    best = jnp.concatenate([best[:, :, :CAPACITY], best[:, :, CAPACITY:]], axis=1)
    best = best.transpose(1, 0, 2)
    best = jnp.concatenate([best[:, :4], best[:, 4:]], axis=2)
    best = jnp.broadcast_to(best[None], (4, 8, 4, 128)).reshape(32, 4, 128)
    best = exchange(best, "xy").reshape(4, 8, 4, 128)
    return pick(place, best).reshape(rows)


def solution(mesh):
    in_specs = (P("dp", None), P("dp"), P("dp"))
    out_specs = P("dp")
    return jax.shard_map(
        on_device, mesh=mesh, in_specs=in_specs, out_specs=out_specs, check_vma=False
    )
```
